32 devices in a mesh: pts: 8 (over z, x), orb: 4 (over y, core).
Axes of the slice: x: 2, y: 2, z: 4, core: 2. Of those that a mesh axis runs over, the one named last changes fastest.
Arguments:
- occ_points: float32 [20480, 1024], P('pts', 'orb'), may hold values from -0.1875 to 0.1875
- vir_points: float32 [20480, 9216], P('pts', 'orb'), may hold values from -0.0625 to 0.0625
- occ_cols: float32 [256, 1024], P('pts', 'orb'), may hold values from -6 to 6
- vir_cols: float32 [256, 9216], P('pts', 'orb'), may hold values from -6 to 6
- occ_energy: float32 [1024], P('orb'), may hold values from -1.5 to -0.2
- vir_energy: float32 [9216], P('orb'), may hold values from 0.2 to 3
- plane_waves: float32 [8192, 20480], P('orb', 'pts'), may hold values from -0.0390625 to 0.0390625
Outputs:
- projected: float32 [2, 8192, 256], P(None, 'orb', 'pts')
The draws below stay inside these ranges and needn't reach their ends.
All inputs are finite; a program needn't handle non-finite values.
Results may differ from the reference program's by a relative error of at most 0.00011.
Values sent between devices are 32-bit elements; how exact they have to be, the bound alone decides.
A program may use at most 128 MiB of HBM per device.

```python
import jax
import jax.numpy as jnp
from jax import lax

NP = 20480
NOCC = 1024
NVIR = 9216
NPW = 8192
COLS = 256


def block_levels(stream_key, dims, cuts, low, high):
    def one(position, blocks):
        heights = jax.random.uniform(jax.random.fold_in(jax.random.fold_in(stream_key, 6), position), (blocks,), jnp.float32, low / len(cuts), high / len(cuts))
        return jnp.repeat(jnp.exp(heights), dims[position] // blocks).reshape((-1,) + (1,) * (len(dims) - position - 1))

    gain = one(*cuts[0])
    for cut in cuts[1:]:
        gain = gain * one(*cut)
    return gain


def normal_values(own_key, extent, spread, most, shards=(), dtype=jnp.bfloat16):
    values = spread * jax.random.normal(own_key, extent, jnp.float32)
    if shards:
        values = values * block_levels(own_key, extent, shards, -0.22, 0.18)
    return jnp.clip(values, -most, most).astype(dtype)


def setup_inputs(seed: int = 0) -> dict:
    streams_of = jax.random.split(jax.random.key(seed), 8)
    occ_points = normal_values(streams_of[0], (NP, NOCC), NOCC ** -0.5, 0.1875, ((0, 8), (1, 4)), jnp.float32)
    vir_points = normal_values(streams_of[1], (NP, NVIR), NVIR ** -0.5, 0.0625, ((0, 8), (1, 4)), jnp.float32)
    occ_cols = normal_values(streams_of[2], (COLS, NOCC), 1.0, 6.0, ((0, 8), (1, 4)), jnp.float32)
    vir_cols = normal_values(streams_of[3], (COLS, NVIR), 1.0, 6.0, ((0, 8), (1, 4)), jnp.float32)
    occ_energy = jnp.clip(-1.5 + 1.3 * jax.random.uniform(streams_of[4], (NOCC,), jnp.float32) ** block_levels(streams_of[4], (NOCC,), ((0, 4),), -0.2, 0.2), -1.5, -0.2)
    vir_energy = jnp.clip(0.2 + 2.8 * jax.random.uniform(streams_of[5], (NVIR,), jnp.float32) ** block_levels(streams_of[5], (NVIR,), ((0, 4),), -0.2, 0.2), 0.2, 3.0)
    plane_waves = normal_values(streams_of[6], (NPW, NP), NP ** -0.5, 0.0390625, ((0, 4), (1, 8)), jnp.float32)
    return {"occ_points": occ_points, "vir_points": vir_points, "occ_cols": occ_cols, "vir_cols": vir_cols, "occ_energy": occ_energy, "vir_energy": vir_energy, "plane_waves": plane_waves}


IMAG_TIMES = (0.3, 1.2)
FREQUENCIES = (0.5, 2.0)
QUAD_WEIGHTS = (0.6, 1.8)


def make_table():
    moments = jnp.array(IMAG_TIMES, jnp.float32)
    omegas = jnp.array(FREQUENCIES, jnp.float32)
    weights = jnp.array(QUAD_WEIGHTS, jnp.float32)
    return 2.0 * weights[None, :] * jnp.cos(omegas[:, None] * moments[None, :])


def contract(left, right):
    return lax.dot_general(left, right, (((1,), (1,)), ((), ())), precision=lax.Precision.HIGHEST, preferred_element_type=jnp.float32)


def reference(occ_points, vir_points, occ_cols, vir_cols, occ_energy, vir_energy, plane_waves):
    moments = jnp.array(IMAG_TIMES, jnp.float32)
    occ_weight = jnp.exp(moments[:, None] * occ_energy[None, :])
    vir_weight = jnp.exp(-moments[:, None] * vir_energy[None, :])
    point_count = occ_points.shape[0]
    columns = occ_cols.shape[0]
    occ_scaled = (occ_cols[None, :, :] * occ_weight[:, None, :]).reshape(2 * columns, -1)
    vir_scaled = (vir_cols[None, :, :] * vir_weight[:, None, :]).reshape(2 * columns, -1)
    occ_green = contract(occ_points, occ_scaled).reshape(point_count, 2, columns)
    vir_green = contract(vir_points, vir_scaled).reshape(point_count, 2, columns)
    response = -(occ_green * vir_green)
    spectral = jnp.einsum('kt,rtc->rkc', make_table(), response, precision=lax.Precision.HIGHEST)
    partial_value = jnp.dot(plane_waves, spectral.reshape(point_count, 2 * columns), precision=lax.Precision.HIGHEST, preferred_element_type=jnp.float32)
    return jnp.transpose(partial_value.reshape(plane_waves.shape[0], 2, columns), (1, 0, 2))
```

```python
import jax
import jax.numpy as jnp
from jax import lax
from jax.sharding import PartitionSpec as P

IMAG_TIMES = (0.3, 1.2)
FREQUENCIES = (0.5, 2.0)
QUAD_WEIGHTS = (0.6, 1.8)
G_SPLIT = 2


def make_table():
    moments = jnp.array(IMAG_TIMES, jnp.float32)
    omegas = jnp.array(FREQUENCIES, jnp.float32)
    weights = jnp.array(QUAD_WEIGHTS, jnp.float32)
    return 2.0 * weights[None, :] * jnp.cos(omegas[:, None] * moments[None, :])


def contract(left, right):
    return lax.dot_general(
        left,
        right,
        (((1,), (1,)), ((), ())),
        precision=lax.Precision.HIGH,
        preferred_element_type=jnp.float32,
    )


def swap(x, axis, bit):
    return lax.ppermute(x, axis, [(i, i ^ bit) for i in range(lax.axis_size(axis))])


def bits_of(count):
    width = count.bit_length() - 1
    return [1 << i for i in reversed(range(width))]


def masks_of(bits):
    masks = [0]
    for bit in bits:
        masks = masks + [m ^ bit for m in masks]
    return masks


def gather(x, axis, bits, dim):
    for bit in bits:
        x = jnp.concatenate([x, swap(x, axis, bit)], axis=dim)
    return x


def scatter_sum(x, axis, bits):
    for bit in reversed(bits):
        half = x.shape[0] // 2
        x = x[:half] + swap(x[half:], axis, bit)
    return x


def weighted(cols, weight):
    value = jnp.transpose(cols, (1, 0, 2, 3))[:, None] * weight[None, :, None, None, :]
    return value.reshape(-1, cols.shape[-1])


def on_device(occ_points, vir_points, occ_cols, vir_cols, occ_energy, vir_energy, plane_waves):
    pts_bits = bits_of(lax.axis_size("pts"))
    orb_bits = bits_of(lax.axis_size("orb"))
    outer, last = pts_bits[:-1], pts_bits[-1]
    orb = lax.axis_index("orb")
    orbs = lax.axis_size("orb")
    orb_masks = masks_of(orb_bits)
    rows = occ_points.shape[0]
    block = occ_cols.shape[0] // orbs
    table = make_table()
    moments = jnp.array(IMAG_TIMES, jnp.float32)
    occ_weight = jnp.exp(moments[:, None] * occ_energy[None, :])
    vir_weight = jnp.exp(-moments[:, None] * vir_energy[None, :])

    def relative(cols):
        cols = cols.reshape(orbs, block, -1)
        parts = [lax.dynamic_index_in_dim(cols, orb ^ m, 0, keepdims=True) for m in orb_masks]
        return jnp.concatenate(parts, axis=0)[None]

    occ_near = gather(relative(occ_cols), "pts", outer, 0)
    occ_far = swap(occ_near, "pts", last)
    vir_near = gather(relative(vir_cols), "pts", outer, 0)
    vir_far = swap(vir_near, "pts", last)
    blocks = vir_near.shape[0]

    def green(points, cols, weight):
        value = contract(weighted(cols, weight), points)
        value = value.reshape(orbs, 2, blocks, block, rows)
        return scatter_sum(value, "orb", orb_bits)[0]

    def spectral(occ, vir):
        response = -(occ * vir)
        parts = [table[k, 0] * response[0] + table[k, 1] * response[1] for k in range(2)]
        value = jnp.stack(parts, axis=1)[:, :, None]
        value = gather(value, "orb", orb_bits, 2)
        return value.reshape(-1, rows)

    occ_near_green = green(occ_points, occ_near, occ_weight)
    occ_far_green = green(occ_points, occ_far, occ_weight)
    vir_near_green = green(vir_points, vir_near, vir_weight)
    vir_far_green = green(vir_points, vir_far, vir_weight)
    spec_far = spectral(occ_far_green, vir_far_green)
    spec_near = spectral(occ_near_green, vir_near_green)

    waves = plane_waves.shape[0] // G_SPLIT
    pieces = [plane_waves[i * waves : (i + 1) * waves] for i in range(G_SPLIT)]
    arrived = [swap(contract(spec_far, piece), "pts", last) for piece in pieces]
    summed = []
    for piece, other in zip(pieces, arrived):
        value = contract(spec_near, piece) + other
        value = value.reshape(blocks, 2, orbs, block, waves)
        summed.append(scatter_sum(value, "pts", outer)[0])
    summed = jnp.concatenate(summed, axis=-1)

    def place(owner):
        apart = orb ^ owner
        width = len(orb_bits)
        return sum(((apart >> i) & 1) << (width - 1 - i) for i in range(width))

    ordered = jnp.stack(
        [lax.dynamic_index_in_dim(summed, place(o), 1, keepdims=False) for o in range(orbs)], axis=1
    )
    return jnp.transpose(ordered.reshape(2, orbs * block, -1), (0, 2, 1))


def solution(mesh):
    in_specs = (
        P("pts", "orb"),
        P("pts", "orb"),
        P("pts", "orb"),
        P("pts", "orb"),
        P("orb"),
        P("orb"),
        P("orb", "pts"),
    )
    out_specs = P(None, "orb", "pts")
    return jax.shard_map(
        on_device, mesh=mesh, in_specs=in_specs, out_specs=out_specs, check_vma=False
    )
```

```python
import jax
import jax.numpy as jnp
from jax import lax
from jax.sharding import PartitionSpec as P

IMAG_TIMES = (0.3, 1.2)
FREQUENCIES = (0.5, 2.0)
QUAD_WEIGHTS = (0.6, 1.8)
G_SPLIT = 4


def make_table():
    moments = jnp.array(IMAG_TIMES, jnp.float32)
    omegas = jnp.array(FREQUENCIES, jnp.float32)
    weights = jnp.array(QUAD_WEIGHTS, jnp.float32)
    return 2.0 * weights[None, :] * jnp.cos(omegas[:, None] * moments[None, :])


def contract(left, right):
    return lax.dot_general(
        left,
        right,
        (((1,), (1,)), ((), ())),
        precision=lax.Precision.HIGH,
        preferred_element_type=jnp.float32,
    )


def swap(x, axis, bit):
    return lax.ppermute(x, axis, [(i, i ^ bit) for i in range(lax.axis_size(axis))])


def bits_of(count):
    width = count.bit_length() - 1
    return [1 << i for i in reversed(range(width))]


def masks_of(bits):
    masks = [0]
    for bit in bits:
        masks = masks + [m ^ bit for m in masks]
    return masks


def gather(x, axis, bits, dim):
    for bit in bits:
        x = jnp.concatenate([x, swap(x, axis, bit)], axis=dim)
    return x


def scatter_sum(x, axis, bits):
    for bit in reversed(bits):
        half = x.shape[0] // 2
        x = x[:half] + swap(x[half:], axis, bit)
    return x


def weighted(cols, weight):
    value = jnp.transpose(cols, (1, 0, 2, 3))[:, None] * weight[None, :, None, None, :]
    return value.reshape(-1, cols.shape[-1])


def on_device(occ_points, vir_points, occ_cols, vir_cols, occ_energy, vir_energy, plane_waves):
    pts_bits = bits_of(lax.axis_size("pts"))
    orb_bits = bits_of(lax.axis_size("orb"))
    outer, last = pts_bits[:-1], pts_bits[-1]
    orb = lax.axis_index("orb")
    orbs = lax.axis_size("orb")
    orb_masks = masks_of(orb_bits)
    rows = occ_points.shape[0]
    block = occ_cols.shape[0] // orbs
    table = make_table()
    moments = jnp.array(IMAG_TIMES, jnp.float32)
    occ_weight = jnp.exp(moments[:, None] * occ_energy[None, :])
    vir_weight = jnp.exp(-moments[:, None] * vir_energy[None, :])

    def relative(cols):
        cols = cols.reshape(orbs, block, -1)
        parts = [lax.dynamic_index_in_dim(cols, orb ^ m, 0, keepdims=True) for m in orb_masks]
        return jnp.concatenate(parts, axis=0)[None]

    def both(cols):
        near = [relative(cols)]
        far = [swap(near[0], "pts", last)]
        for bit in outer:
            sent = near[0] if len(near) == 1 else jnp.concatenate(near, axis=0)
            near.append(swap(sent, "pts", bit))
            far.append(swap(near[-1], "pts", last))
        return jnp.concatenate(near, axis=0), jnp.concatenate(far, axis=0)

    occ_near, occ_far = both(occ_cols)
    vir_near, vir_far = both(vir_cols)
    blocks = vir_near.shape[0]
    half = rows // 2

    def halved(value):
        value = value.reshape(orbs, 2, blocks, block, -1)
        return scatter_sum(value, "orb", orb_bits[-1:])

    def total(value):
        return scatter_sum(value, "orb", orb_bits[:-1])[0]

    def spectral(occ, vir):
        response = -(occ * vir)
        parts = [table[k, 0] * response[0] + table[k, 1] * response[1] for k in range(2)]
        return jnp.stack(parts, axis=1)[:, :, None]

    barrier = lax.optimization_barrier
    occ_first = [halved(contract(weighted(c, occ_weight), occ_points)) for c in (occ_near, occ_far)]
    vir_near, *occ_first = barrier((vir_near, *occ_first))
    near_cols = weighted(vir_near, vir_weight)
    occ_near_green = total(occ_first[0])
    occ_far_green = total(occ_first[1])
    near_one = halved(contract(near_cols, vir_points[:half]))
    near_cols, occ_near_green = barrier((near_cols, occ_near_green))
    near_two = halved(contract(near_cols, vir_points[half:]))
    vir_far, near_one = barrier((vir_far, near_one))
    far_cols = weighted(vir_far, vir_weight)
    far_one = halved(contract(far_cols, vir_points[:half]))
    far_cols, near_two, occ_far_green = barrier((far_cols, near_two, occ_far_green))
    far_two = halved(contract(far_cols, vir_points[half:]))
    vir_near_green = jnp.concatenate([total(near_one), total(near_two)], axis=-1)
    far_one, far_two, vir_near_green = barrier((far_one, far_two, vir_near_green))
    vir_far_green = jnp.concatenate([total(far_one), total(far_two)], axis=-1)
    spec_far = spectral(occ_far_green, vir_far_green)
    spec_far = gather(spec_far, "orb", orb_bits, 2).reshape(-1, rows)
    vir_near_green, spec_far = barrier((vir_near_green, spec_far))
    spec_near = gather(spectral(occ_near_green, vir_near_green), "orb", orb_bits[:-1], 2)

    waves = plane_waves.shape[0] // G_SPLIT
    pieces = [plane_waves[i * waves : (i + 1) * waves] for i in range(G_SPLIT)]
    sent = [contract(spec_far, piece) for piece in pieces]
    arrived = [swap(value, "pts", last) for value in sent]
    spec_near, arrived[0] = barrier((spec_near, arrived[0]))
    spec_near = gather(spec_near, "orb", orb_bits[-1:], 2).reshape(-1, rows)
    own = [barrier(contract(spec_near, piece)) for piece in pieces]
    summed = []
    for value, other in zip(own, arrived):
        value = (value + other).reshape(blocks, 2, orbs, block, waves)
        summed.append(scatter_sum(value, "pts", outer)[0])
    summed = jnp.concatenate(summed, axis=-1)

    def place(owner):
        apart = orb ^ owner
        width = len(orb_bits)
        return sum(((apart >> i) & 1) << (width - 1 - i) for i in range(width))

    ordered = jnp.stack(
        [lax.dynamic_index_in_dim(summed, place(o), 1, keepdims=False) for o in range(orbs)], axis=1
    )
    return jnp.transpose(ordered.reshape(2, orbs * block, -1), (0, 2, 1))


def solution(mesh):
    in_specs = (
        P("pts", "orb"),
        P("pts", "orb"),
        P("pts", "orb"),
        P("pts", "orb"),
        P("orb"),
        P("orb"),
        P("orb", "pts"),
    )
    out_specs = P(None, "orb", "pts")
    return jax.shard_map(
        on_device, mesh=mesh, in_specs=in_specs, out_specs=out_specs, check_vma=False
    )
```
